32 devices in a mesh: tm: 8 (over z, core), space: 4 (over y, x).
Axes of the slice: x: 2, y: 2, z: 4, core: 2. Of those that a mesh axis runs over, the one named last changes fastest.
Arguments:
- increment: float32 [8, 4, 137, 512], P('tm', None, None, 'space'), may hold values from -26 to 26
- courant: float32 [8, 4, 137, 512], P('tm', None, None, 'space'), may hold values from -0.9 to 0.9
- error_weight: float32 [4, 137], replicated, may hold values from 0.5 to 2
- obs_code: int32 [8, 4, 4, 128], P('tm', 'space'), may hold values from 0 to 280574, as said below
- obs_values: float32 [8, 4, 4, 3, 128], P('tm', 'space'), as said below
- obs_count: int32 [8, 4, 4], P('tm', 'space'), may hold values from 25 to 128, as said below
Outputs:
- new_increment: float32 [8, 4, 137, 512], P('tm', None, None, 'space')
- departures: float32 [8, 4, 4, 128], P('tm', 'space')
The draws below stay inside these ranges and needn't reach their ends.
Inputs may be any that keep to these rules, and one draw needn't show every extreme that they name: `obs_code`: code = ((t * 4 + f) * 137 + l) * 128 + c for an observation of the state after step t + 1 of its sub-window, field f, level l, between columns c and c + 1 of the destination tile, c < 127; slots at or beyond the count carry no observation. `obs_values`: row 1 lies in [0, 1], row 2 in [0.5, 4]. `obs_count`: in every sub-window some destination tile receives 128 observations from every source tile.
All inputs are finite; a program needn't handle non-finite values.
Results may differ from the reference program's by a relative error of at most 0.0003.
Values sent between devices are 32-bit elements; how exact they have to be, the bound alone decides.
A program may use at most 64 MiB of HBM per device.

```python
import math
import jax
import jax.numpy as jnp
from jax import lax

NF = 4
LEV = 137
CD = 128
STEPS = 4
CAP = 128
NWIN = 8
NS = 4
NCOL = 512


def draw_increment(key, part):
    key = jax.random.fold_in(key, 11)
    first = jax.random.fold_in(key, 0)
    shape = (NWIN, NF, LEV, NCOL)
    rise = 1.0 + 2.0 * jnp.arange(NWIN, dtype=jnp.float32) / max(NWIN - 1, 1)
    rise = rise[:, None, None, None]
    base = jnp.clip(jax.random.normal(first, shape, jnp.float32), -6.0, 6.0)
    return base * rise


def draw_obs_code(key, part):
    key = jax.random.fold_in(key, 23)
    keys = jax.random.split(key, 4)
    shape = (NWIN, NS, NS, CAP)
    when = jax.random.randint(keys[0], shape, 0, STEPS)
    field = jax.random.randint(keys[1], shape, 0, NF)
    level = jax.random.randint(keys[2], shape, 0, LEV)
    column = jax.random.randint(keys[3], shape, 0, CD - 1)
    code = ((when * NF + field) * LEV + level) * CD + column
    code = code.at[0, 0, 0, 0].set(STEPS * NF * LEV * CD - 2)
    code = code.at[0, 0, 0, 1].set(0)
    return code.astype(jnp.int32)


def draw_obs_count(key, part):
    key = jax.random.fold_in(key, 37)
    first, second = jax.random.split(key)
    base = jax.random.randint(first, (NWIN, NS, NS), max(2, CAP // 5), CAP // 2 + 1)
    heavy = jax.random.randint(second, (NWIN,), 0, NS)
    target = jnp.arange(NS, dtype=jnp.int32)[None, None, :] == heavy[:, None, None]
    return jnp.where(target, CAP, base).astype(jnp.int32)


def draw_obs_values(key, part):
    key = jax.random.fold_in(key, 51)
    keys = jax.random.split(key, 3)
    shape = (NWIN, NS, NS, 1, CAP)
    innovation = jnp.clip(jax.random.normal(keys[0], shape, jnp.float32), -6.0, 6.0)
    weight = jax.random.uniform(keys[1], shape, jnp.float32, 0.0, 1.0)
    rinv = jnp.exp(jax.random.uniform(keys[2], shape, jnp.float32, math.log(0.5), math.log(4.0)))
    return jnp.concatenate([innovation, weight, rinv], axis=3)


def level_of(own_key, dims, shards, smallest, high):
    def one(position, blocks):
        heights = jax.random.uniform(jax.random.fold_in(jax.random.fold_in(own_key, 6), position), (blocks,), jnp.float32, smallest / len(shards), high / len(shards))
        return jnp.repeat(jnp.exp(heights), dims[position] // blocks).reshape((-1,) + (1,) * (len(dims) - position - 1))

    loudness = one(*shards[0])
    for cut in shards[1:]:
        loudness = loudness * one(*cut)
    return loudness


def setup_inputs(seed: int = 0) -> dict:
    key_list = jax.random.split(jax.random.key(seed), 7)
    return {
        "increment": draw_increment(jax.random.fold_in(key_list[6], 71), 0),
        "courant": jnp.clip(jax.random.uniform(key_list[1], (NWIN, STEPS, LEV, NCOL), jnp.float32, -0.9, 0.9) * level_of(key_list[1], (NWIN, STEPS, LEV, NCOL), ((0, 8), (3, 4)), -0.4, 0.0), -0.9, 0.9),
        "error_weight": jnp.clip(jnp.exp(jax.random.uniform(key_list[2], (NF, LEV), jnp.float32, math.log(0.5), math.log(2.0))), 0.5, 2.0),
        "obs_code": draw_obs_code(jax.random.fold_in(key_list[6], 71), 0),
        "obs_values": draw_obs_values(jax.random.fold_in(key_list[6], 71), 0),
        "obs_count": draw_obs_count(jax.random.fold_in(key_list[6], 71), 0),
    }


def coefficients(cour):
    left = 0.5 * cour * (1.0 + cour)
    centre = 1.0 - cour * cour
    right = 0.5 * cour * (cour - 1.0)
    return left, centre, right


def tangent(start, cour, flat, when, weight):
    left, centre, right = coefficients(cour)

    def one(carry, n):
        state, seen_all = carry
        state = centre[n] * state + left[n] * jnp.roll(state, 1, axis=-1) + right[n] * jnp.roll(state, -1, axis=-1)
        line = state.reshape(-1)
        seen = weight * line[flat] + (1.0 - weight) * line[flat + 1]
        seen_all = jnp.where(when == n, seen, seen_all)
        return (state, seen_all), None

    init = (start, jnp.zeros(flat.shape, jnp.float32))
    (state, seen_all), _ = lax.scan(one, init, jnp.arange(STEPS, dtype=jnp.int32))
    return state, seen_all


def adjoint(carried, cour, flat, when, weight, pushed):
    left, centre, right = coefficients(cour)

    def inject(lam, n):
        mass = jnp.where(when == n, pushed, 0.0)
        line = lam.reshape(-1)
        line = line.at[flat].add(weight * mass).at[flat + 1].add((1.0 - weight) * mass)
        return line.reshape(lam.shape)

    lam = inject(-carried, STEPS - 1)

    def one(lam, n):
        lam = centre[n] * lam + jnp.roll(left[n] * lam, -1, axis=-1) + jnp.roll(right[n] * lam, 1, axis=-1)
        return inject(lam, n - 1), None

    lam, _ = lax.scan(one, lam, jnp.arange(STEPS, dtype=jnp.int32), reverse=True)
    return lam


def reference(increment, courant, error_weight, obs_code, obs_values, obs_count):
    per_state = NF * LEV * CD
    flat_local = obs_code % per_state
    when = obs_code // per_state
    column = flat_local % CD
    row = flat_local // CD
    owner = jnp.arange(NS, dtype=jnp.int32)[None, None, :, None]
    flat = row * NCOL + owner * CD + column
    innovation = obs_values[:, :, :, 0, :]
    weight = obs_values[:, :, :, 1, :]
    rinv = obs_values[:, :, :, 2, :]
    valid = jnp.arange(CAP, dtype=jnp.int32)[None, None, None, :] < obs_count[:, :, :, None]
    ends, seen = lax.map(lambda a: tangent(*a), (increment, courant, flat, when, weight))
    departures = jnp.where(valid, seen - innovation, 0.0)
    pushed = rinv * departures
    previous = jnp.concatenate([jnp.zeros_like(ends[:1]), ends[:-1]], axis=0)
    jump = increment - previous
    weighted = error_weight[None, :, :, None] * jump
    following = jnp.concatenate([weighted[1:], jnp.zeros_like(weighted[:1])], axis=0)
    lam = lax.map(lambda a: adjoint(*a), (following, courant, flat, when, weight, pushed))
    gradient = weighted + lam
    cost = 0.5 * (jnp.sum(weighted * jump) + jnp.sum(pushed * departures))
    norm = jnp.sum(gradient * gradient)
    new_increment = increment - (cost / norm) * gradient
    return new_increment, departures
```

```python
import functools
import jax
import jax.numpy as jnp
from jax import lax
from jax.experimental import pallas as pl
from jax.experimental.pallas import tpu as pltpu
from jax.sharding import PartitionSpec as P

MESH = pl.DeviceIdType.MESH
LANES = 128
GATHER_PARTS = 3
SCATTER_PARTS = 2


def split(value, parts):
    out = []
    for part in range(parts):
        piece = value.astype(jnp.bfloat16)
        out.append(piece)
        if part + 1 < parts:
            value = value - piece.astype(jnp.float32)
    return out


def kernel(
    nt, ns, nf, lev, steps, inc_ref, cour_ref, ew_ref, code_ref, val_ref, cnt_ref,
    out_ref, dep_ref,
    xc, rem, ew_pad, edges, obs_out, obs_in, onehot, weights, parts, pieces, forcing,
    end, prev, nxt, grad, spill, spill_in, dep_out, dep_in, sums, sums_in, totals, totals_in,
    edge_s, edge_r, obs_s, obs_r, nxt_s, nxt_r, prev_s, prev_r, spill_s, spill_r,
    dep_s, dep_r, sum_s, sum_r, tot_s, tot_r,
):
    cd = LANES
    tiles = nf + 1
    wide = tiles * LANES
    gap = LANES // nf
    extra = lev - LANES
    per_state = nf * lev * cd
    slots = ns * LANES
    ring = cd + 8
    k = lax.axis_index("tm")
    me = lax.axis_index("space")
    f32 = jnp.float32

    def space_peer(i):
        return lax.rem(me + i, ns)

    def tm_peer(i):
        return lax.rem(k + i, nt)

    barrier = pltpu.get_barrier_semaphore()
    for i in range(1, ns):
        pl.semaphore_signal(barrier, inc=1, device_id=(k, space_peer(i)), device_id_type=MESH)
    for i in range(1, nt):
        pl.semaphore_signal(barrier, inc=1, device_id=(tm_peer(i), me), device_id_type=MESH)

    rem[...] = jnp.zeros_like(rem)
    for f in range(nf):
        rem[0, f * gap : f * gap + extra, :] = inc_ref[0, f, LANES:lev, :]
        for n in range(steps):
            rem[1 + n, f * gap : f * gap + extra, :] = cour_ref[0, n, LANES:lev, :]
    for f in range(nf):
        xc[f, 0:cd, :] = inc_ref[0, f, 0:LANES, :].T
    xc[nf, 0:cd, :] = rem[0].T
    for n in range(steps):
        xc[tiles + n, 0:cd, :] = cour_ref[0, n, 0:LANES, :].T
        xc[tiles + steps + n, 0:cd, :] = rem[1 + n].T
    lane_row = lax.broadcasted_iota(jnp.int32, (1, LANES), 1)
    for d in range(ns):
        used = lane_row < cnt_ref[0, 0, d]
        obs_out[d, 0:1, :] = jnp.where(used, code_ref[0, 0, d : d + 1, :], -1).astype(f32)
        obs_out[d, 1:4, :] = val_ref[0, 0, d]

    pl.semaphore_wait(barrier, ns - 1 + nt - 1)

    def remote(src, dst, send, recv, target):
        return pltpu.make_async_remote_copy(
            src_ref=src, dst_ref=dst, send_sem=send, recv_sem=recv,
            device_id=target, device_id_type=MESH,
        )

    left, right = space_peer(ns - 1), space_peer(1)
    edge_copies = [
        remote(xc.at[:, 0:8, :], edges.at[0], edge_s.at[0], edge_r.at[0], (k, left)),
        remote(xc.at[:, cd - 8 : cd, :], edges.at[1], edge_s.at[1], edge_r.at[1], (k, right)),
    ]
    obs_copies = [
        remote(
            obs_out.at[space_peer(i)], obs_in.at[me], obs_s.at[i], obs_r.at[i], (k, space_peer(i))
        )
        for i in range(1, ns)
    ]
    for copy in obs_copies + edge_copies:
        copy.start()
    not_first, not_last = k > 0, k < nt - 1
    before, after = lax.max(k - 1, 0), lax.min(k + 1, nt - 1)
    nxt_copy = remote(
        xc.at[0:tiles, 0:cd, :], nxt, nxt_s.at[0], nxt_r.at[0], (before, me)
    )

    @pl.when(not_first)
    def _():
        nxt_copy.start()

    @pl.when(jnp.logical_not(not_last))
    def _():
        nxt[...] = jnp.zeros_like(nxt)

    @pl.when(jnp.logical_not(not_first))
    def _():
        prev[...] = jnp.zeros_like(prev)

    obs_in[me] = obs_out[me]
    ew_pad[...] = jnp.zeros_like(ew_pad)
    for f in range(nf):
        ew_pad[f : f + 1, 0:extra] = ew_ref[f : f + 1, LANES:lev]
    ew_rows = [ew_ref[f : f + 1, 0:LANES] for f in range(nf)]
    ew_last = ew_pad[0:1, :]
    for f in range(1, nf):
        ew_last = ew_last + pltpu.roll(ew_pad[f : f + 1, :], f * gap, 1)
    ew_rows.append(ew_last)

    for copy in obs_copies:
        copy.wait_recv()

    def gathered(row):
        return jnp.concatenate([obs_in[s, row : row + 1, :] for s in range(ns)], axis=1)

    code = gathered(0).astype(jnp.int32)
    innovation, weight, rinv = gathered(1), gathered(2), gathered(3)
    when = jnp.zeros_like(code)
    for n in range(1, steps):
        when = when + (code >= n * per_state).astype(jnp.int32)
    flat = code - when * per_state
    row = lax.shift_right_arithmetic(flat, 7)
    column = jnp.bitwise_and(flat, LANES - 1)
    field = jnp.zeros_like(code)
    for f in range(1, nf):
        field = field + (row >= f * lev).astype(jnp.int32)
    level = row - field * lev
    place = jnp.where(
        level < LANES, field * LANES + level, nf * LANES + field * gap + level - LANES
    )
    key = when * wide + place
    line = lax.broadcasted_iota(jnp.int32, (LANES, LANES), 0)
    for s in range(ns):
        block = slice(s * LANES, (s + 1) * LANES)
        key_s = key[:, block]
        for t in range(steps * tiles):
            hit = line == key_s - t * LANES
            onehot[t * LANES : (t + 1) * LANES, block] = jnp.where(hit, 1.0, 0.0).astype(
                jnp.bfloat16
            )
        col_s, w_s = column[:, block], weight[:, block]
        weights[:, block] = jnp.where(line == col_s, w_s, 0.0) + jnp.where(
            line == col_s + 1, 1.0 - w_s, 0.0
        )

    for copy in edge_copies:
        copy.wait_recv()
    sub = lax.broadcasted_iota(jnp.int32, (8, LANES), 0)
    for t in range(tiles + 2 * steps):
        xc[t, cd:ring, :] = jnp.where(sub < 4, edges[0, t], edges[1, t])

    def courant_of(t, n):
        return xc[tiles + n if t < nf else tiles + steps + n]

    prev_copies = []
    for t in range(tiles):
        x = xc[t]
        for n in range(steps):
            c = courant_of(t, n)
            lower = pltpu.roll(x, 1, 0)
            upper = pltpu.roll(x, ring - 1, 0)
            x = x + (0.5 * c) * ((lower - upper) + c * ((lower + upper) - 2.0 * x))
            at = (n * tiles + t) * LANES
            for p, piece in enumerate(split(x[0:cd], GATHER_PARTS)):
                parts[p * cd : (p + 1) * cd, at : at + LANES] = piece
        end[t] = x[0:cd]
        copy = remote(end.at[t], prev.at[t], prev_s.at[t], prev_r.at[t], (after, me))
        prev_copies.append(copy)
        pl.when(not_last)(copy.start)

    seen_parts = jnp.dot(parts[...], onehot[...], preferred_element_type=f32)
    seen = seen_parts[0:cd]
    for p in range(1, GATHER_PARTS):
        seen = seen + seen_parts[p * cd : (p + 1) * cd]
    hx = jnp.sum(seen * weights[...], axis=0, keepdims=True)
    departed = jnp.where(code >= 0, hx - innovation, 0.0)
    pushed = rinv * departed
    for s in range(ns):
        dep_out[s, 0:1, :] = departed[:, s * LANES : (s + 1) * LANES]
    dep_copies = [
        remote(
            dep_out.at[space_peer(i)], dep_in.at[me], dep_s.at[i], dep_r.at[i], (k, space_peer(i))
        )
        for i in range(1, ns)
    ]
    for copy in dep_copies:
        copy.start()
    dep_in[me] = dep_out[me]
    for p, piece in enumerate(split(weights[...] * pushed, SCATTER_PARTS)):
        pieces[p * cd : (p + 1) * cd, :] = piece
    for n in range(steps):
        part = lax.dot_general(
            pieces[...],
            onehot[n * wide : (n + 1) * wide, :],
            (((1,), (1,)), ((), ())),
            preferred_element_type=f32,
        )
        total = part[0:cd]
        for p in range(1, SCATTER_PARTS):
            total = total + part[p * cd : (p + 1) * cd]
        forcing[n] = total

    pl.when(not_last)(nxt_copy.wait_recv)
    share = jnp.where(not_last, 1.0, 0.0)
    for t in range(tiles):
        lanes = slice(t * LANES, (t + 1) * LANES)
        own = forcing[steps - 1, :, lanes] - (share * ew_rows[t]) * (nxt[t] - end[t])
        lam = jnp.concatenate([own, jnp.zeros((8, LANES), f32)], axis=0)
        for n in reversed(range(steps)):
            c = courant_of(t, n)
            u = (0.5 * c) * lam
            v = c * u
            lam = (lam - 2.0 * v) + (pltpu.roll(u + v, ring - 1, 0) + pltpu.roll(v - u, 1, 0))
            if n > 0:
                lam = jnp.concatenate(
                    [lam[0:cd] + forcing[n - 1, :, lanes], lam[cd:ring]], axis=0
                )
        grad[t] = lam[0:cd]
        spill[t] = lam[cd:ring]
    spill_copies = [
        remote(spill, spill_in.at[0], spill_s.at[0], spill_r.at[0], (k, left)),
        remote(spill, spill_in.at[1], spill_s.at[1], spill_r.at[1], (k, right)),
    ]
    for copy in spill_copies:
        copy.start()

    def folded(value):
        return jnp.sum(value.reshape(-1, 8, LANES), axis=0)

    cost = jnp.zeros((8, LANES), f32)
    norm = jnp.zeros((8, LANES), f32)
    for t in range(tiles):
        pl.when(not_first)(prev_copies[t].wait_recv)
        jump = xc[t, 0:cd, :] - prev[t]
        weighted = ew_rows[t] * jump
        cost = cost + folded(weighted * jump)
        g = grad[t] + weighted
        grad[t] = g
        inner = g[8 : cd - 8]
        norm = norm + folded(inner * inner)
    obs_cost = jnp.zeros((1, LANES), f32)
    for s in range(ns):
        block = slice(s * LANES, (s + 1) * LANES)
        obs_cost = obs_cost + pushed[:, block] * departed[:, block]
    sums[0] = cost + jnp.where(sub == 0, obs_cost, 0.0)
    for copy in spill_copies:
        copy.wait_recv()
    for t in range(tiles):
        low = grad[t, 0:8, :] + jnp.where(sub < 4, spill_in[1, t], 0.0)
        high = grad[t, cd - 8 : cd, :] + jnp.where(sub < 4, 0.0, spill_in[0, t])
        grad[t, 0:8, :] = low
        grad[t, cd - 8 : cd, :] = high
        norm = norm + (low * low + high * high)
    sums[1] = norm

    sum_copies = [
        remote(sums, sums_in.at[i], sum_s.at[i], sum_r.at[i], (k, space_peer(i)))
        for i in range(1, ns)
    ]
    for copy in sum_copies:
        copy.start()
    for t in range(tiles):
        grad[t] = grad[t].T
    for copy in sum_copies:
        copy.wait_recv()
    total = sums[...]
    for i in range(1, ns):
        total = total + sums_in[i]
    totals[...] = total
    total_copies = [
        remote(totals, totals_in.at[i], tot_s.at[i], tot_r.at[i], (tm_peer(i), me))
        for i in range(1, nt)
    ]
    for copy in total_copies:
        copy.start()
    for copy in dep_copies:
        copy.wait_recv()
    for d in range(ns):
        dep_ref[0, 0, d : d + 1, :] = dep_in[d, 0:1, :]
    for copy in edge_copies + obs_copies + dep_copies + spill_copies + sum_copies:
        copy.wait_send()
    pl.when(not_first)(nxt_copy.wait_send)
    for copy in prev_copies:
        pl.when(not_last)(copy.wait_send)
    for copy in total_copies:
        copy.wait_recv()
    total = totals[...]
    for i in range(1, nt):
        total = total + totals_in[i]
    flat_total = jnp.sum(jnp.sum(total, axis=1, keepdims=True), axis=2, keepdims=True)
    ratio = 0.5 * flat_total[0] / flat_total[1]
    for f in range(nf):
        out_ref[0, f, 0:LANES, :] = inc_ref[0, f, 0:LANES, :] - ratio * grad[f]
        out_ref[0, f, LANES:lev, :] = (
            inc_ref[0, f, LANES:lev, :] - ratio * grad[nf, f * gap : f * gap + extra, :]
        )
    for copy in total_copies:
        copy.wait_send()


def solution(mesh):
    nt, ns = mesh.shape["tm"], mesh.shape["space"]
    in_specs = (
        P("tm", None, None, "space"),
        P("tm", None, None, "space"),
        P(),
        P("tm", "space", None, None),
        P("tm", "space", None, None, None),
        P("tm", "space", None),
    )
    out_specs = (P("tm", None, None, "space"), P("tm", "space", None, None))

    def on_device(increment, courant, error_weight, obs_code, obs_values, obs_count):
        _, nf, lev, cd = increment.shape
        steps = courant.shape[1]
        tiles = nf + 1
        wide = tiles * LANES
        slots = ns * LANES
        f32, bf16 = jnp.float32, jnp.bfloat16
        vmem = pl.BlockSpec(memory_space=pltpu.VMEM)
        dma = pltpu.SemaphoreType.DMA
        state = pltpu.VMEM((tiles, cd, LANES), f32)
        return pl.pallas_call(
            functools.partial(kernel, nt, ns, nf, lev, steps),
            out_shape=(
                jax.ShapeDtypeStruct(increment.shape, f32),
                jax.ShapeDtypeStruct(obs_code.shape, f32),
            ),
            in_specs=[vmem] * 5 + [pl.BlockSpec(memory_space=pltpu.SMEM)],
            out_specs=(vmem, vmem),
            scratch_shapes=[
                pltpu.VMEM((tiles + 2 * steps, cd + 8, LANES), f32),
                pltpu.VMEM((1 + steps, LANES, LANES), f32),
                pltpu.VMEM((8, LANES), f32),
                pltpu.VMEM((2, tiles + 2 * steps, 8, LANES), f32),
                pltpu.VMEM((ns, 8, LANES), f32),
                pltpu.VMEM((ns, 8, LANES), f32),
                pltpu.VMEM((steps * wide, slots), bf16),
                pltpu.VMEM((cd, slots), f32),
                pltpu.VMEM((GATHER_PARTS * cd, steps * wide), bf16),
                pltpu.VMEM((SCATTER_PARTS * cd, slots), bf16),
                pltpu.VMEM((steps, cd, wide), f32),
                state,
                state,
                state,
                state,
                pltpu.VMEM((tiles, 8, LANES), f32),
                pltpu.VMEM((2, tiles, 8, LANES), f32),
                pltpu.VMEM((ns, 8, LANES), f32),
                pltpu.VMEM((ns, 8, LANES), f32),
                pltpu.VMEM((2, 8, LANES), f32),
                pltpu.VMEM((ns, 2, 8, LANES), f32),
                pltpu.VMEM((2, 8, LANES), f32),
                pltpu.VMEM((nt, 2, 8, LANES), f32),
                dma((2,)), dma((2,)),
                dma((ns,)), dma((ns,)),
                dma((1,)), dma((1,)),
                dma((tiles,)), dma((tiles,)),
                dma((2,)), dma((2,)),
                dma((ns,)), dma((ns,)),
                dma((ns,)), dma((ns,)),
                dma((nt,)), dma((nt,)),
            ],
            compiler_params=pltpu.CompilerParams(
                collective_id=0, has_side_effects=True, vmem_limit_bytes=40 * 1024 * 1024
            ),
        )(increment, courant, error_weight, obs_code, obs_values, obs_count)

    return jax.shard_map(
        on_device, mesh=mesh, in_specs=in_specs, out_specs=out_specs, check_vma=False
    )
```
